256 devices in a mesh: section: 8 (over x, z_hi), dp: 4 (over y), tp: 8 (over z_lo, core).
Axes of the slice: x: 4, y: 4, z: 8 (z_hi: 2, z_lo: 4; z = z_hi * 4 + z_lo), core: 2. Of those that a mesh axis runs over, the one named last changes fastest.
Arguments:
- features: bfloat16 [16, 512, 8192], P('section', 'dp', 'tp'), may hold values from -6 to 6
- selected: int32 [3], replicated, may hold values from 0 to 15, as said below
- target_hidden: bfloat16 [512, 8192], P('dp', ('section', 'tp')), may hold values from -6 to 6
- unite_weight: bfloat16 [3, 8192, 8192], P(None, 'tp', 'section')
- head_weight: bfloat16 [65536, 8192], P(('section', 'tp'), 'dp')
Outputs:
- unite_grad: bfloat16 [3, 8192, 8192], P(None, 'tp', ('section', 'dp'))
- kl_loss: float32 [512], P('dp')
The draws below stay inside these ranges and needn't reach their ends.
Inputs may be any that keep to these rules, and one draw needn't show every extreme that they name: The entries of selected are distinct, and the last one is the deepest offered layer, 15.
All inputs are finite; a program needn't handle non-finite values.
Results may differ from the reference program's by a relative error of at most 0.015.
Values may be sent and summed in bfloat16 or wider, within the bound.
A program may use at most 128 MiB of HBM per device.

```python
import jax
import jax.numpy as jnp
from jax import lax

D = 8192
LAYERS = 3
TOK = 128
TOKENS = 512
VOCAB = 65536
EXPORTS = 16
N_DP = 4


def draw_selected(key, part):
    key = jax.random.fold_in(key, 37)
    order = jax.random.permutation(key, EXPORTS - 1)
    lower = order[:LAYERS - 1].astype(jnp.int32)
    deepest = jnp.full((1,), EXPORTS - 1, jnp.int32)
    return jnp.concatenate([lower, deepest]).astype(jnp.int32)


def draw_unite_weight(key, part):
    key = jax.random.fold_in(key, 11)
    base_key, col_key = jax.random.split(key)
    column = jnp.arange(D, dtype=jnp.float32) / D
    base = jax.random.normal(base_key, (LAYERS, D, D), jnp.float32)
    spread = 0.6 * column + 0.4 * jax.random.uniform(col_key, (D,), jnp.float32)
    scale = jnp.power(10.0, spread) / (LAYERS * D) ** 0.5
    return (base * scale).astype(jnp.bfloat16)


def draw_head_weight(key, part):
    key = jax.random.fold_in(key, 23)
    base_key = jax.random.fold_in(key, 0)
    row_pos = jnp.arange(VOCAB, dtype=jnp.float32)[:, None] / VOCAB
    scale = (3.0 + 1.5 * row_pos) / D ** 0.5
    base = jax.random.normal(base_key, (VOCAB, D), jnp.float32) * scale
    return base.astype(jnp.bfloat16)


def block_levels(rng, dims, cuts, smallest, high):
    def one(dim, blocks):
        steps = jax.random.uniform(jax.random.fold_in(jax.random.fold_in(rng, 6), dim), (blocks,), jnp.float32, smallest / len(cuts), high / len(cuts))
        return jnp.repeat(jnp.exp(steps), dims[dim] // blocks).reshape((-1,) + (1,) * (len(dims) - dim - 1))

    gain = one(*cuts[0])
    for cut in cuts[1:]:
        gain = gain * one(*cut)
    return gain


def normal_values(key, dims, scale, bound, cuts=(), kind=jnp.bfloat16):
    entries = scale * jax.random.normal(key, dims, jnp.float32)
    if cuts:
        entries = entries * block_levels(key, dims, cuts, -0.22, 0.18)
    return jnp.clip(entries, -bound, bound).astype(kind)


def setup_inputs(seed: int = 0) -> dict:
    splits = jax.random.split(jax.random.key(seed), 6)
    features = normal_values(splits[0], (EXPORTS, TOKENS, D), 1.0, 6.0, ((0, 8), (1, 4), (2, 8)))
    selected = draw_selected(jax.random.fold_in(splits[5], 71), 0)
    target_hidden = normal_values(splits[2], (TOKENS, D), 1.0, 6.0, ((0, 4), (1, 64)))
    unite_weight = draw_unite_weight(jax.random.fold_in(splits[5], 71), 0)
    head_weight = draw_head_weight(jax.random.fold_in(splits[5], 71), 0)
    return dict(features=features, selected=selected, target_hidden=target_hidden, unite_weight=unite_weight, head_weight=head_weight)


EPS = 1e-05

def contract_rows(left, right):
    return lax.dot_general(left, right, (((1,), (1,)), ((), ())), preferred_element_type=jnp.float32)

def log_soft(logits):
    peak = lax.optimization_barrier(jnp.max(logits, axis=1, keepdims=True))
    return logits - peak - jnp.log(lax.optimization_barrier(jnp.sum(jnp.exp(logits - peak), axis=1, keepdims=True)))

def reference(features, selected, target_hidden, unite_weight, head_weight):
    united = jnp.zeros((TOKENS, D), jnp.float32)
    picked = []
    for position in range(LAYERS):
        chosen_layer = jnp.take(features, selected[position], axis=0)
        picked.append(chosen_layer)
        united = united + jnp.dot(chosen_layer, unite_weight[position], preferred_element_type=jnp.float32)
    scale_inv = lax.rsqrt(lax.optimization_barrier(jnp.mean(united * united, axis=1, keepdims=True)) + EPS)
    hidden = (united * scale_inv).astype(jnp.bfloat16)
    target_log = log_soft(contract_rows(target_hidden, head_weight))
    draft_log = log_soft(contract_rows(hidden, head_weight))
    target_prob = jnp.exp(target_log)
    draft_prob = jnp.exp(draft_log)
    kl_loss = lax.optimization_barrier(jnp.sum(target_prob * (target_log - draft_log), axis=1))
    delta_logits = (draft_prob - target_prob).astype(jnp.bfloat16)
    back_cols = jnp.dot(delta_logits, head_weight, preferred_element_type=jnp.float32)
    dot_sums = lax.optimization_barrier(jnp.sum(back_cols * united, axis=1, keepdims=True))
    grad_united = (scale_inv * back_cols - united * scale_inv ** 3 * dot_sums / D).astype(jnp.bfloat16)
    gradients = []
    for position in range(LAYERS):
        accum = jnp.zeros((D, D), jnp.float32)
        for group in range(N_DP):
            rows_lo = group * TOK
            part_grad = jnp.dot(picked[position][rows_lo:rows_lo + TOK].T, grad_united[rows_lo:rows_lo + TOK], preferred_element_type=jnp.float32)
            part_grad = lax.optimization_barrier(part_grad.astype(jnp.bfloat16)).astype(jnp.float32)
            accum = accum + part_grad
        gradients.append(accum.astype(jnp.bfloat16))
    return (jnp.stack(gradients), kl_loss)
```

```python
import jax
import jax.numpy as jnp
from jax import lax
from jax.experimental import pallas as pl
from jax.experimental.pallas import tpu as pltpu
from jax.sharding import PartitionSpec as P

D = 8192
LAYERS = 3
EPS = 1e-05
BF = jnp.bfloat16
F32 = jnp.float32
NSEM = 256


def nt(a, b):
    return lax.dot_general(a, b, (((1,), (1,)), ((), ())), preferred_element_type=F32)


def nn(a, b):
    return jnp.dot(a, b, preferred_element_type=F32)


def rows_to_cols(tile):
    return jnp.concatenate([tile, jnp.zeros((120, 128), F32)], axis=0).T


def combine(parts):
    row = lax.broadcasted_iota(jnp.int32, (8, 128), 0)
    upper = row < 4

    def spread(p):
        return jnp.where(upper, p[0:1, :], p[4:5, :])

    peaks = [spread(p) for p in parts]
    peak = peaks[0]
    for other in peaks[1:]:
        peak = jnp.maximum(peak, other)
    total = jnp.zeros((8, 128), F32)
    for p, mine in zip(parts, peaks):
        total = total + p * jnp.exp(mine - peak)
    return jnp.where((row == 0) | (row == 4), peak, total)


def kernel(
    sel, feat_h, tgt_h, w_h, head_h, out_h, kl_o,
    feat, tgt, w, head, msk, fx, fs, fz, fall, ft,
    part, pc, pz, uni, ssc, ssz, ssa, ssx, scol, tcol,
    h_t, h_d, lp_t, lp_d, lq_t, lq_d, rq_t, rq_d, sm, sq_t, sq_d, rs_t, rs_d,
    zt, zd, stat, stc, stz, stx, fin, fcol, dall,
    bk, rc, bx, rx, rz, bs, ur, gcol, gu, outv,
    lsem, send, recv,
):
    sec = lax.axis_index("section")
    y = lax.axis_index("dp")
    tp = lax.axis_index("tp")
    x, zh = lax.div(sec, 2), lax.rem(sec, 2)
    zl, c = lax.div(tp, 2), lax.rem(tp, 2)
    z = zh * 4 + zl
    oc = 1 - c

    def mod4(v):
        return lax.rem(v + 8, 4)

    def to_x(v):
        return {"section": v * 2 + zh}

    def to_y(v):
        return {"dp": v}

    def to_z(v):
        return {"section": x * 2 + lax.div(v, 4), "tp": lax.rem(v, 4) * 2 + c}

    sibling = {"tp": zl * 2 + oc}
    across = {"section": y * 2 + zh, "dp": x}

    def across_z(v):
        return {"section": y * 2 + lax.div(v, 4), "dp": x, "tp": lax.rem(v, 4) * 2 + c}

    def turned(h):
        return {"section": y * 2 + zh, "dp": zl, "tp": x * 2 + h}

    def turned_back(h):
        return {"section": zl * 2 + zh, "dp": x, "tp": y * 2 + h}

    counter = [0]

    def sems(n):
        base = counter[0]
        counter[0] += n
        assert counter[0] <= NSEM
        return base

    ends = []

    def copy(src, dst, sem, dev, rsem=None):
        return pltpu.make_async_remote_copy(
            src_ref=src, dst_ref=dst, send_sem=send.at[sem],
            recv_sem=recv.at[sem if rsem is None else rsem],
            device_id=dev, device_id_type=pl.DeviceIdType.MESH,
        )

    def push(src, dst, sem, dev, rsem=None, when=None):
        if when is None:
            copy(src, dst, sem, dev, rsem).start()
            ends.append(lambda: copy(src, dst, sem, dev, rsem).wait_send())
        else:
            def go():
                copy(src, dst, sem, dev, rsem).start()

            def end():
                copy(src, dst, sem, dev, rsem).wait_send()

            pl.when(when)(go)
            ends.append(lambda: pl.when(when)(end))

    def await_recv(dst, sem, when=None):
        def go():
            copy(dst, dst, 0, sibling, sem).wait_recv()

        if when is None:
            go()
        else:
            pl.when(when)(go)

    def m(v, k):
        return pl.multiple_of(v, k)

    half_c = pl.ds(m(c * 128, 128), 128)
    half_o = pl.ds(m(oc * 128, 128), 128)

    loads = [
        pltpu.make_async_copy(feat_h, feat, lsem.at[0]),
        pltpu.make_async_copy(tgt_h, tgt, lsem.at[1]),
        pltpu.make_async_copy(w_h, w, lsem.at[2]),
        pltpu.make_async_copy(head_h, head, lsem.at[3]),
    ]
    for load in loads:
        load.start()

    barrier = pltpu.get_barrier_semaphore()

    def greet(dev):
        pl.semaphore_signal(barrier, inc=1, device_id=dev, device_id_type=pl.DeviceIdType.MESH)

    for d in range(1, 4):
        greet(to_x(mod4(x + d)))
        greet(to_y(mod4(y + d)))
    for d in range(1, 8):
        greet(to_z(lax.rem(z + d, 8)))
    greet(sibling)
    off_x = x != y
    off_z = jnp.logical_or(off_x, y != zl)

    @pl.when(off_x)
    def _():
        for v in range(8):
            greet(across_z(v))

    @pl.when(off_z)
    def _():
        for h in range(2):
            greet(turned(h))
            greet(turned_back(h))

    pl.semaphore_wait(
        barrier, 14 + jnp.where(off_x, 8, 0) + jnp.where(off_z, 4, 0)
    )

    class Gather:
        def __init__(self, hid, own):
            self.hid, self.own = hid, own
            self.s1, self.sz, self.sx = sems(1), sems(8), sems(8)
            self.so, self.sf = sems(2), sems(8)

        def turn(self):
            hid, own = self.hid, self.own
            push(own, hid.at[y, z, :, half_c], self.s1, across, when=off_x)

            @pl.when(jnp.logical_not(off_x))
            def _():
                hid[x, z, :, half_c] = own[...]

        def along_z(self):
            hid = self.hid
            mine = hid.at[x, z, :, half_c]
            if self.own is not None:
                await_recv(mine, self.s1, when=off_x)
            for d in range(1, 8):
                push(mine, mine, self.sz + d, to_z(lax.rem(z + d, 8)))

        def along_x(self, g):
            hid = self.hid
            base = zh * 4 if g == 0 else 4 - zh * 4
            for j in range(1 if g == 0 else 0, 4):
                zz = base + mod4(zl + j)
                await_recv(hid.at[x, zz, :, half_c], self.sz + lax.rem(z - zz + 8, 8))
            block = hid.at[x, pl.ds(base, 4), :, half_c]
            for d in (1, 3, 2):
                push(block, block, self.sx + g * 4 + d, to_x(mod4(x + d)))
            push(block, block, self.so + g, sibling)

        def over(self, g):
            hid = self.hid
            base = zh * 4 if g == 0 else 4 - zh * 4
            for d in (1, 3, 2):
                block = hid.at[mod4(x - d), pl.ds(base, 4), :, half_c]
                await_recv(block, self.sx + g * 4 + d)
                push(block, block, self.sf + g * 4 + d, sibling)

        def finish(self):
            hid = self.hid
            for g in range(2):
                base = zh * 4 if g == 0 else 4 - zh * 4
                await_recv(hid.at[x, pl.ds(base, 4), :, half_o], self.so + g)
                for d in (1, 3, 2):
                    block = hid.at[mod4(x - d), pl.ds(base, 4), :, half_o]
                    await_recv(block, self.sf + g * 4 + d)

    class Logits:
        def __init__(self, hid, lp, lq, rq, sq, rs):
            self.hid, self.lp, self.lq, self.rq, self.sq, self.rs = hid, lp, lq, rq, sq, rs
            self.s, self.ss = sems(4), sems(4)

        def product(self, rels):
            hid, lp = self.hid, self.lp

            @pl.loop(0, 4)
            def _(n):
                cols = pl.ds(m(n * 256, 256), 256)
                left = jnp.concatenate(
                    [jnp.concatenate([hid[mod4(y + rel), i] for i in range(8)], axis=1) for rel in rels],
                    axis=0,
                )
                out = nt(left, head[cols, :])
                for j, rel in enumerate(rels):
                    lp[rel, :, cols] = out[j * 128:(j + 1) * 128]

        def send(self, rel):
            lp, lq, sq = self.lp, self.lq, self.sq

            @pl.loop(0, 4)
            def _(i):
                rows = pl.ds(m(i * 32, 32), 32)
                v = lp[rel, rows]
                peak = jnp.maximum(jnp.max(jnp.abs(v), axis=1, keepdims=True), 1e-30)
                lq[rel, rows] = jnp.round(v * (32767.0 / peak)).astype(jnp.int32).astype(jnp.int16)
                sm[rows] = jnp.broadcast_to(peak / 32767.0, (32, 128))

            sq[rel] = sm[...].T[0:8]
            dev = to_y(mod4(y + rel))
            push(lq.at[rel], self.rq.at[rel], self.s + rel, dev)
            push(sq.at[rel], self.rs.at[rel], self.ss + rel, dev)

        def finish(self, col, other):
            for rel in (1, 3, 2):
                await_recv(self.rs.at[rel], self.ss + rel)
            row = lax.broadcasted_iota(jnp.int32, (8, 128), 0)
            tile = other
            for rel in (1, 3, 2):
                tile = jnp.where(row == rel, self.rs[rel], tile)
            col[...] = rows_to_cols(tile)
            for rel in (1, 3, 2):
                await_recv(self.rq.at[rel], self.s + rel)

        def total(self, col, rows):
            out = self.lp[0, rows]
            for rel in (1, 3, 2):
                part_sum = self.rq[rel, rows].astype(jnp.int32).astype(F32)
                out = out + part_sum * col[rows, rel:rel + 1]
            return out

    target = Gather(h_t, tgt)
    draft = Gather(h_d, None)
    logits_t = Logits(h_t, lp_t, lq_t, rq_t, sq_t, rs_t)
    logits_d = Logits(h_d, lp_d, lq_d, rq_d, sq_d, rs_d)

    loads[1].wait()
    target.turn()
    loads[0].wait()
    f1, f2, f3, f4, f5 = sems(12), sems(3), sems(12), sems(12), sems(12)
    for k in range(LAYERS):
        chosen = sel[k]
        value = feat[lax.rem(chosen, 2)]
        mine = lax.div(chosen, 2) == sec
        msk[k] = jnp.where(mine, value, jnp.zeros_like(value))
        for d in (1, 3, 2):
            xx = mod4(x + d)
            push(msk.at[k, pl.ds(m(xx * 32, 32), 32)], fx.at[k, d - 1], f1 + k * 4 + d, to_x(xx))
    quarter = pl.ds(m(x * 32, 32), 32)
    other_zh = {"section": x * 2 + 1 - zh}
    for k in range(LAYERS):
        for d in (1, 3, 2):
            await_recv(fx.at[k, d - 1], f1 + k * 4 + d)
        fs[k] = msk[k, quarter] + fx[k, 0] + fx[k, 1] + fx[k, 2]
        push(fs.at[k], fz.at[k], f2 + k, other_zh)
    target.along_z()
    for k in range(LAYERS):
        await_recv(fz.at[k], f2 + k)
        fall[y, k, quarter] = fs[k] + fz[k]
        block = fall.at[y, k, quarter]
        for d in (1, 3, 2):
            push(block, block, f3 + k * 4 + d, to_x(mod4(x + d)))
            push(block, block, f4 + k * 4 + d, to_y(mod4(y + d)))

    loads[2].wait()
    for k in range(LAYERS):
        for d in (1, 3, 2):
            xx = mod4(x - d)
            await_recv(fall.at[y, k, pl.ds(m(xx * 32, 32), 32)], f3 + k * 4 + d)
        if k == LAYERS - 1:
            target.along_x(0)
            target.along_x(1)

        @pl.loop(0, 4)
        def _(n, k=k):
            cols = pl.ds(m(n * 256, 256), 256)
            term = nn(fall[y, k], w[k, :, cols])
            if k:
                part[n, 0] = part[n, 0] + term[:, :128]
                part[n, 1] = part[n, 1] + term[:, 128:]
            else:
                part[n, 0] = term[:, :128]
                part[n, 1] = term[:, 128:]

    r1, r2 = sems(1), sems(4)
    push(part.at[:, oc], pc, r1, sibling)
    await_recv(pc, r1)
    for d in (2, 1, 3, 0):
        v = mod4(zl + d)
        part[v, c] = part[v, c] + pc[v]
        remote = off_x if d == 0 else None
        push(part.at[v, c], pz.at[zl], r2 + d, across_z(zh * 4 + v), rsem=r2 + zl, when=remote)

    @pl.when(jnp.logical_not(off_x))
    def _():
        pz[zl] = part[zl, c]

    for d in range(4):
        v = mod4(zl + d)
        await_recv(pz.at[v], r2 + v, when=off_x if d == 0 else None)
    uni[...] = pz[0] + pz[1] + pz[2] + pz[3]
    h_d[x, z, :, half_c] = uni[...].astype(BF)
    draft.along_z()
    s_c, s_z, s_a, s_x = sems(1), sems(8), sems(1), sems(4)
    squares = jnp.sum(uni[...] * uni[...], axis=1, keepdims=True)
    ssc[0] = jnp.broadcast_to(squares, (128, 128)).T[0:8]
    push(ssc.at[0], ssc.at[1], s_c, sibling)
    t2 = sems(2)
    for h in range(2):
        src = uni.at[pl.ds(h * 64, 64), :]
        push(src, ur.at[:, half_c], t2 + h, turned(h), rsem=t2 + c,
             when=jnp.logical_or(off_z, c != h))

    @pl.when(jnp.logical_not(off_z))
    def _():
        ur[:, half_c] = uni[pl.ds(m(c * 64, 64), 64), :]

    target.over(0)
    target.over(1)
    await_recv(ssc.at[1], s_c)
    ssz[0] = ssc[0] + ssc[1]
    for d in range(1, 8):
        push(ssz.at[0], ssz.at[d], s_z + d, to_z(lax.rem(z + d, 8)))
    draft.along_x(0)
    draft.along_x(1)
    target.finish()
    loads[3].wait()
    logits_t.product((1, 3, 2, 0))
    for rel in (2, 1, 3):
        logits_t.send(rel)
    for d in range(1, 8):
        await_recv(ssz.at[d], s_z + d)
    total = ssz[0]
    for d in range(1, 8):
        total = total + ssz[d]
    ssa[0] = total
    push(ssa.at[0], ssa.at[1], s_a, across, when=off_x)
    draft.over(0)
    draft.over(1)
    await_recv(ssa.at[1], s_a, when=off_x)
    ssx[0] = jnp.where(off_x, ssa[1], ssa[0])
    for d in range(1, 4):
        push(ssx.at[0], ssx.at[d], s_x + d, to_x(mod4(x + d)))
    draft.finish()
    for e in (1, 3, 2):
        yy = mod4(y - e)
        for k in range(LAYERS):
            await_recv(fall.at[yy, k, quarter], f4 + k * 4 + e)
        block = fall.at[yy, :, quarter]
        for d in (1, 3, 2):
            push(block, block, f5 + (e - 1) * 4 + d, to_x(mod4(x + d)))
    logits_d.product((1, 3))
    logits_d.send(1)
    logits_d.send(3)
    logits_d.product((2, 0))
    logits_d.send(2)
    def transpose(b):
        @pl.loop(0, LAYERS)
        def _(k):
            for i in range(4):
                ft[k, pl.ds(i * 256, 256), pl.ds(m(b * 128, 128), 128)] = fall[b, k, :, pl.ds(i * 256, 256)].T

    transpose(y)
    logits_t.finish(tcol, jnp.zeros((8, 128), F32))

    @pl.loop(0, 4)
    def _(i):
        rows = pl.ds(m(i * 32, 32), 32)
        zt[rows] = logits_t.total(tcol, rows)

    for d in range(1, 4):
        await_recv(ssx.at[d], s_x + d)
    scale_rows = lax.rsqrt((ssx[0] + ssx[1] + ssx[2] + ssx[3]) / D + EPS)
    logits_d.finish(scol, scale_rows)

    @pl.loop(0, 4)
    def _(i):
        rows = pl.ds(m(i * 32, 32), 32)
        a = zt[rows]
        b = logits_d.total(scol, rows) * scol[rows, 0:1]
        zd[rows] = b
        ma = jnp.max(a, axis=1, keepdims=True)
        mb = jnp.max(b, axis=1, keepdims=True)
        ea, eb = jnp.exp(a - ma), jnp.exp(b - mb)

        def total(v):
            return jnp.sum(v, axis=1, keepdims=True)

        values = [ma, total(ea), total(ea * (a - b)), total(ea * b), mb, total(eb), total(eb * b)]
        spot = lax.broadcasted_iota(jnp.int32, (32, 128), 1)
        out = jnp.zeros((32, 128), F32)
        for j, v in enumerate(values):
            out = jnp.where(spot == j, v, out)
        stat[rows] = out

    q_c, q_z, q_x, q_y = sems(1), sems(8), sems(4), sems(4)
    stc[0] = stat[...].T[0:8]
    push(stc.at[0], stc.at[1], q_c, sibling)
    await_recv(stc.at[1], q_c)
    stz[0] = combine([stc[0], stc[1]])
    for d in range(1, 8):
        push(stz.at[0], stz.at[d], q_z + d, to_z(lax.rem(z + d, 8)))
    for d in range(1, 8):
        await_recv(stz.at[d], q_z + d)
    stx[0] = combine([stz[d] for d in range(8)])
    for d in range(1, 4):
        push(stx.at[0], stx.at[d], q_x + d, to_x(mod4(x + d)))
    for d in range(1, 4):
        await_recv(stx.at[d], q_x + d)
    all_stats = combine([stx[d] for d in range(4)])
    log_t = all_stats[0:1] + jnp.log(all_stats[1:2])
    log_d = all_stats[4:5] + jnp.log(all_stats[5:6])
    kl_o[...] = all_stats[2:3] / all_stats[1:2] - log_t + log_d
    energy = all_stats[6:7] / all_stats[5:6] - all_stats[3:4] / all_stats[1:2]
    row = lax.broadcasted_iota(jnp.int32, (8, 128), 0)
    tile = jnp.where(row == 0, log_t, jnp.where(row == 1, log_d, jnp.where(row == 2, scale_rows[0:1], energy)))
    fin[y] = tile
    fcol[...] = rows_to_cols(tile)

    @pl.loop(0, 4)
    def _(i):
        rows = pl.ds(m(i * 32, 32), 32)
        pt = jnp.exp(zt[rows] - fcol[rows, 0:1])
        pd = jnp.exp(zd[rows] - fcol[rows, 1:2])
        dall[y, rows] = (pd - pt).astype(BF)

    d1 = sems(4)
    for d in (1, 3, 2):
        push(dall.at[y], dall.at[y], d1 + d, to_y(mod4(y + d)))
    for d in range(1, 4):
        push(fin.at[y], fin.at[y], q_y + d, to_y(mod4(y + d)))

    b_c, b_x, b_z = sems(4), sems(16), sems(8)

    def product(rels):
        for rel in rels:
            if rel:
                b = mod4(y + rel)
                await_recv(dall.at[b], d1 + 4 - rel)

        @pl.loop(0, 8)
        def _(n):
            cols = pl.ds(m(n * 256, 256), 256)
            left = jnp.concatenate([dall[mod4(y + rel)] for rel in rels], axis=0)
            out = nn(left, head[:, cols]).astype(BF)
            for j, rel in enumerate(rels):
                bk[rel, :, cols] = out[j * 128:(j + 1) * 128]

        for rel in rels:
            push(bk.at[rel, pl.ds(m(oc * 64, 64), 64)], rc.at[rel], b_c + rel, sibling)

    def over_core(rel):
        await_recv(rc.at[rel], b_c + rel)
        mine = pl.ds(m(c * 64, 64), 64)
        for n in range(8):
            cols = pl.ds(n * 256, 256)
            s = bk[rel, mine, cols].astype(F32) + rc[rel, :, cols].astype(F32)
            bx[rel, n % 4, n // 4] = s.astype(BF)
        for d in (1, 3, 2):
            xx = mod4(x + d)
            push(bx.at[rel, xx], rx.at[rel, d - 1], b_x + rel * 4 + d, to_x(xx))

    def over_x(rel):
        b = mod4(y + rel)
        for d in (1, 3, 2):
            await_recv(rx.at[rel, d - 1], b_x + rel * 4 + d)
        s = bx[rel, x].astype(F32)
        for d in range(3):
            s = s + rx[rel, d].astype(F32)
        bs[rel] = s.astype(BF)
        for g in range(2):
            zz = g * 4 + b
            push(bs.at[rel, g], rz.at[z], b_z + rel * 2 + g, across_z(zz), rsem=b_z + z,
                 when=jnp.logical_or(off_x, zz != z))

            @pl.when(jnp.logical_not(jnp.logical_or(off_x, zz != z)))
            def _():
                rz[z] = bs[rel, g]

    product((0,))
    over_core(0)
    product((1, 3))
    over_core(1)
    over_core(3)
    over_x(0)
    product((2,))
    over_core(2)
    over_x(1)
    over_x(3)
    over_x(2)

    for d in range(1, 4):
        await_recv(fin.at[mod4(y - d)], q_y + d)
    gcol[...] = rows_to_cols(fin[zl])
    await_recv(ur.at[:, pl.ds(0, 128)], t2, when=jnp.logical_or(off_z, c != 0))
    await_recv(ur.at[:, pl.ds(128, 128)], t2 + 1, when=jnp.logical_or(off_z, c != 1))
    for e in (1, 3, 2):
        yy = mod4(y - e)
        for d in (1, 3, 2):
            xx = mod4(x - d)
            await_recv(fall.at[yy, :, pl.ds(m(xx * 32, 32), 32)], f5 + (e - 1) * 4 + d)
        transpose(yy)
    for d in range(8):
        zz = lax.rem(z + d, 8)
        await_recv(rz.at[zz], b_z + zz, when=off_x if d == 0 else None)
    bt = rz[0].astype(F32)
    for j in range(1, 8):
        bt = bt + rz[j].astype(F32)
    mine = pl.ds(m(c * 64, 64), 64)
    scale = gcol[mine, 2:3]
    gu[zl, c] = (scale * (bt - ur[...] * (scale * gcol[mine, 3:4] / D))).astype(BF)

    g1, g2 = sems(4), sems(4)
    for d in (0, 1, 3, 2):
        if d:
            block = gu.at[zl, c]
            push(block, block, g1 + d, {"tp": mod4(zl + d) * 2 + c})
    for d in (0, 1, 3, 2):
        v = mod4(zl - d)
        block = gu.at[v, c]
        if d:
            await_recv(block, g1 + d)
        push(block, block, g2 + d, sibling)
    for d in (0, 1, 3, 2):
        await_recv(gu.at[mod4(zl - d), oc], g2 + d)

    stores = []
    for k in range(LAYERS):
        @pl.loop(0, 4)
        def _(i, k=k):
            rows = pl.ds(m(i * 256, 256), 256)
            right = jnp.concatenate([gu[b, h] for b in range(4) for h in range(2)], axis=0)
            outv[k, rows] = nn(ft[k, rows], right).astype(BF)

        store = pltpu.make_async_copy(outv.at[k], out_h.at[k], lsem.at[4 + k])
        store.start()
        stores.append(store)
    for end in ends:
        end()
    for store in stores:
        store.wait()


def per_device(features, selected, target_hidden, unite_weight, head_weight):
    def vm(shape, kind):
        return pltpu.VMEM(shape, kind)

    scratch = [
        vm((2, 128, 1024), BF), vm((128, 128), BF), vm((3, 1024, 1024), BF), vm((1024, 2048), BF),
        vm((3, 128, 1024), BF), vm((3, 3, 32, 1024), BF), vm((3, 32, 1024), BF), vm((3, 32, 1024), BF),
        vm((4, 3, 128, 1024), BF), vm((3, 1024, 512), BF),
        vm((4, 2, 128, 128), F32), vm((4, 128, 128), F32), vm((4, 128, 128), F32), vm((128, 128), F32),
        vm((2, 8, 128), F32), vm((8, 8, 128), F32), vm((2, 8, 128), F32), vm((4, 8, 128), F32),
        vm((128, 128), F32), vm((128, 128), F32),
        vm((4, 8, 128, 256), BF), vm((4, 8, 128, 256), BF),
        vm((4, 128, 1024), F32), vm((4, 128, 1024), F32),
        vm((4, 128, 1024), jnp.int16), vm((4, 128, 1024), jnp.int16),
        vm((4, 128, 1024), jnp.int16), vm((4, 128, 1024), jnp.int16), vm((128, 128), F32),
        vm((4, 8, 128), F32), vm((4, 8, 128), F32), vm((4, 8, 128), F32), vm((4, 8, 128), F32),
        vm((128, 1024), F32), vm((128, 1024), F32), vm((128, 128), F32),
        vm((2, 8, 128), F32), vm((8, 8, 128), F32), vm((4, 8, 128), F32),
        vm((4, 8, 128), F32), vm((128, 128), F32), vm((4, 128, 1024), BF),
        vm((4, 128, 2048), BF), vm((4, 64, 2048), BF), vm((4, 4, 2, 64, 256), BF),
        vm((4, 3, 2, 64, 256), BF), vm((8, 64, 256), BF), vm((4, 2, 64, 256), BF),
        vm((64, 256), F32), vm((128, 128), F32),
        vm((4, 2, 64, 256), BF), vm((3, 1024, 256), BF),
        pltpu.SemaphoreType.DMA((8,)), pltpu.SemaphoreType.DMA((NSEM,)), pltpu.SemaphoreType.DMA((NSEM,)),
    ]
    anywhere = pl.BlockSpec(memory_space=pl.ANY)
    grad, loss = pl.pallas_call(
        kernel,
        out_shape=(
            jax.ShapeDtypeStruct((3, 1024, 256), BF),
            jax.ShapeDtypeStruct((1, 128), F32),
        ),
        in_specs=[pl.BlockSpec(memory_space=pltpu.SMEM)] + [anywhere] * 4,
        out_specs=(anywhere, pl.BlockSpec(memory_space=pltpu.VMEM)),
        scratch_shapes=scratch,
        compiler_params=pltpu.CompilerParams(
            collective_id=0, has_side_effects=True, vmem_limit_bytes=58 * 1024 * 1024
        ),
    )(selected, features, target_hidden, unite_weight, head_weight)
    return grad, loss.reshape(128)


def solution(mesh):
    placed = (
        P("section", "dp", "tp"),
        P(),
        P("dp", ("section", "tp")),
        P(None, "tp", "section"),
        P(("section", "tp"), "dp"),
    )
    return jax.shard_map(
        per_device,
        mesh=mesh,
        in_specs=placed,
        out_specs=(P(None, "tp", ("section", "dp")), P("dp")),
        check_vma=False,
    )
```

```python
import jax
import jax.numpy as jnp
from jax import lax
from jax.experimental import pallas as pl
from jax.experimental.pallas import tpu as pltpu
from jax.sharding import PartitionSpec as P

D = 8192
LAYERS = 3
EPS = 1e-05
BF = jnp.bfloat16
F32 = jnp.float32
NSEM = 256


def nt(a, b):
    return lax.dot_general(a, b, (((1,), (1,)), ((), ())), preferred_element_type=F32)


def nn(a, b):
    return jnp.dot(a, b, preferred_element_type=F32)


def rows_to_cols(tile):
    return jnp.concatenate([tile, jnp.zeros((120, 128), F32)], axis=0).T


def combine(parts):
    row = lax.broadcasted_iota(jnp.int32, (8, 128), 0)
    upper = row < 4

    def spread(p):
        return jnp.where(upper, p[0:1, :], p[4:5, :])

    peaks = [spread(p) for p in parts]
    peak = peaks[0]
    for other in peaks[1:]:
        peak = jnp.maximum(peak, other)
    total = jnp.zeros((8, 128), F32)
    for p, mine in zip(parts, peaks):
        total = total + p * jnp.exp(mine - peak)
    return jnp.where((row == 0) | (row == 4), peak, total)


def kernel(
    sel, feat_h, tgt_h, w_h, head_h, ft_h, gu_h, kl_o,
    feat, tgt, w, head, msk, fx, fs, fz, fall, ft,
    part, pc, pz, uni, ssc, ssz, ssa, ssx, scol, tcol,
    h_t, h_d, lp_t, lp_d, lq_t, lq_d, rq_t, rq_d, sm, sq_t, sq_d, rs_t, rs_d,
    zt, zd, stat, stc, stz, stx, ste, fin, fcol, dall,
    bk, rc, bx, rx, rz, bs, bsum, bturn, ur, gcol, gu,
    lsem, send, recv,
):
    sec = lax.axis_index("section")
    y = lax.axis_index("dp")
    tp = lax.axis_index("tp")
    x, zh = lax.div(sec, 2), lax.rem(sec, 2)
    zl, c = lax.div(tp, 2), lax.rem(tp, 2)
    z = zh * 4 + zl
    oc = 1 - c

    def mod4(v):
        return lax.rem(v + 8, 4)

    def to_x(v):
        return {"section": v * 2 + zh}

    def to_y(v):
        return {"dp": v}

    def to_z(v):
        return {"section": x * 2 + lax.div(v, 4), "tp": lax.rem(v, 4) * 2 + c}

    sibling = {"tp": zl * 2 + oc}
    group = mod4(x - y)

    def there(v):
        return {"section": mod4(x + y) * 2 + lax.div(v, 4), "dp": x, "tp": lax.rem(v, 4) * 2 + c}

    def back_to(v):
        return {"section": y * 2 + lax.div(v, 4), "dp": group, "tp": lax.rem(v, 4) * 2 + c}

    def far(d, j):
        zz = lax.rem(z + c + 2 * j, 8)
        return {"section": mod4(x + d) * 2 + lax.div(zz, 4), "tp": lax.rem(zz, 4) * 2 + c}

    def turned(h):
        return {"section": y * 2 + zh, "dp": zl, "tp": group * 2 + h}

    def turned_back(h):
        return {"section": mod4(x + zl) * 2 + zh, "dp": x, "tp": y * 2 + h}

    counter = [0]

    def sems(n):
        base = counter[0]
        counter[0] += n
        assert counter[0] <= NSEM
        return base

    ends = []

    def copy(src, dst, sem, dev, rsem=None):
        return pltpu.make_async_remote_copy(
            src_ref=src, dst_ref=dst, send_sem=send.at[sem],
            recv_sem=recv.at[sem if rsem is None else rsem],
            device_id=dev, device_id_type=pl.DeviceIdType.MESH,
        )

    def push(src, dst, sem, dev, rsem=None, when=None):
        if when is None:
            copy(src, dst, sem, dev, rsem).start()
            ends.append(lambda: copy(src, dst, sem, dev, rsem).wait_send())
        else:
            def go():
                copy(src, dst, sem, dev, rsem).start()

            def end():
                copy(src, dst, sem, dev, rsem).wait_send()

            pl.when(when)(go)
            ends.append(lambda: pl.when(when)(end))

    def await_recv(dst, sem, when=None):
        def go():
            copy(dst, dst, 0, sibling, sem).wait_recv()

        if when is None:
            go()
        else:
            pl.when(when)(go)

    def m(v, k):
        return pl.multiple_of(v, k)

    half_c = pl.ds(m(c * 128, 128), 128)
    half_o = pl.ds(m(oc * 128, 128), 128)

    loads = [
        pltpu.make_async_copy(feat_h, feat, lsem.at[0]),
        pltpu.make_async_copy(tgt_h, tgt, lsem.at[1]),
        pltpu.make_async_copy(w_h, w, lsem.at[2]),
        pltpu.make_async_copy(head_h, head, lsem.at[3]),
    ]
    for load in loads:
        load.start()

    barrier = pltpu.get_barrier_semaphore()

    def greet(dev):
        pl.semaphore_signal(barrier, inc=1, device_id=dev, device_id_type=pl.DeviceIdType.MESH)

    for d in range(1, 4):
        greet(to_x(mod4(x + d)))
        greet(to_y(mod4(y + d)))
    for d in range(1, 8):
        greet(to_z(lax.rem(z + d, 8)))
    greet(sibling)
    off_x = jnp.logical_or(x != 0, y != 0)
    off_z = jnp.logical_or(off_x, zl != 0)

    @pl.when(off_x)
    def _():
        for v in range(4):
            greet(there(zh * 4 + v))
            greet(back_to(zh * 4 + v))

    @pl.when(off_z)
    def _():
        for h in range(2):
            greet(turned(h))
            greet(turned_back(h))

    @pl.when(c == 0)
    def _():
        for d in range(1, 4):
            for j in range(1, 4):
                greet(far(d, j))

    @pl.when(c == 1)
    def _():
        for d in range(1, 4):
            for j in range(4):
                greet(far(d, j))

    pl.semaphore_wait(
        barrier, 23 + 3 * c + jnp.where(off_x, 8, 0) + jnp.where(off_z, 4, 0)
    )

    class Gather:
        def __init__(self, hid, own):
            self.hid, self.own = hid, own
            self.s1, self.sz, self.sx = sems(1), sems(8), sems(8)
            self.so, self.sf = sems(2), sems(8)
            self.s2, self.sz2 = sems(1), sems(8)

        def turn(self):
            hid, own = self.hid, self.own
            push(own, hid.at[y, z, :, half_c], self.s1, there(z), when=off_x)

            @pl.when(jnp.logical_not(off_x))
            def _():
                hid[group, z, :, half_c] = own[...]

        def along_z(self):
            mine = self.hid.at[group, z, :, half_c]
            if self.own is not None:
                await_recv(mine, self.s1, when=off_x)
            for d in range(1, 8):
                push(mine, mine, self.sz + d, to_z(lax.rem(z + d, 8)))

        def hop(self):
            piece = self.hid.at[group, z, :, half_c]
            push(piece, piece, self.s2, to_x(mod4(x + 2)))

        def hop_z(self):
            piece = self.hid.at[mod4(group + 2), z, :, half_c]
            await_recv(piece, self.s2)
            for d in range(1, 8):
                push(piece, piece, self.sz2 + d, to_z(lax.rem(z + d, 8)))

        def hop_over(self):
            for d in range(1, 8):
                await_recv(self.hid.at[mod4(group + 2), lax.rem(z + 8 - d, 8), :, half_c], self.sz2 + d)
            for g in range(2):
                block = self.block(2, g, half_c)
                push(block, block, self.sf + g * 4 + 2, sibling)

        def block(self, e, g, half):
            base = zh * 4 if g == 0 else 4 - zh * 4
            return self.hid.at[mod4(group + e), pl.ds(base, 4), :, half]

        def await_z(self, g):
            base = zh * 4 if g == 0 else 4 - zh * 4
            for j in range(1 if g == 0 else 0, 4):
                zz = base + mod4(zl + j)
                await_recv(self.hid.at[group, zz, :, half_c], self.sz + lax.rem(z - zz + 8, 8))

        def along_x(self, g, steps):
            block = self.block(0, g, half_c)
            for d in steps:
                push(block, block, self.sx + g * 4 + d, to_x(mod4(x + d)))

        def own_over(self, g):
            block = self.block(0, g, half_c)
            push(block, block, self.so + g, sibling)

        def over(self, g, e):
            block = self.block(e, g, half_c)
            await_recv(block, self.sx + g * 4 + 4 - e)
            push(block, block, self.sf + g * 4 + e, sibling)

        def finish(self, e):
            for g in range(2):
                await_recv(self.block(e, g, half_o), self.sf + g * 4 + e if e else self.so + g)

    class Logits:
        def __init__(self, hid, lp, lq, rq, sq, rs):
            self.hid, self.lp, self.lq, self.rq, self.sq, self.rs = hid, lp, lq, rq, sq, rs
            self.s, self.ss = sems(4), sems(4)

        def product(self, steps):
            hid, lp = self.hid, self.lp

            @pl.loop(0, 4)
            def _(n):
                cols = pl.ds(m(n * 256, 256), 256)
                left = jnp.concatenate(
                    [jnp.concatenate([hid[mod4(group + e), i] for i in range(8)], axis=1) for e in steps],
                    axis=0,
                )
                out = nt(left, head[cols, :])
                for j, e in enumerate(steps):
                    lp[e, :, cols] = out[j * 128:(j + 1) * 128]

        def send(self, e):
            lp, lq, sq = self.lp, self.lq, self.sq
            b = mod4(group + e)

            @pl.when(b != y)
            def _():
                @pl.loop(0, 4)
                def _(i):
                    rows = pl.ds(m(i * 32, 32), 32)
                    v = lp[e, rows]
                    peak = jnp.maximum(jnp.max(jnp.abs(v), axis=1, keepdims=True), 1e-30)
                    lq[e, rows] = jnp.round(v * (32767.0 / peak)).astype(jnp.int32).astype(jnp.int16)
                    sm[rows] = jnp.broadcast_to(peak / 32767.0, (32, 128))

                sq[e] = sm[...].T[0:8]

            push(lq.at[e], self.rq.at[y], self.s + e, to_y(b), rsem=self.s + y, when=b != y)
            push(sq.at[e], self.rs.at[y], self.ss + e, to_y(b), rsem=self.ss + y, when=b != y)

        def finish(self, col, other):
            row = lax.broadcasted_iota(jnp.int32, (8, 128), 0)
            tile = other
            for e in (1, 3, 2):
                yy = mod4(y - e)
                await_recv(self.rs.at[yy], self.ss + yy)
                tile = jnp.where(row == e, self.rs[yy], tile)
            col[...] = rows_to_cols(tile)
            for e in (1, 3, 2):
                yy = mod4(y - e)
                await_recv(self.rq.at[yy], self.s + yy)

        def total(self, col, rows):
            out = self.lp[mod4(y - group), rows]
            for e in (1, 3, 2):
                term = self.rq[mod4(y - e), rows].astype(jnp.int32).astype(F32)
                out = out + term * col[rows, e:e + 1]
            return out

    target = Gather(h_t, tgt)
    draft = Gather(h_d, None)
    logits_t = Logits(h_t, lp_t, lq_t, rq_t, sq_t, rs_t)
    logits_d = Logits(h_d, lp_d, lq_d, rq_d, sq_d, rs_d)

    loads[1].wait()
    target.turn()
    loads[0].wait()
    f1, f2, f3, f4, f5 = sems(12), sems(3), sems(12), sems(12), sems(12)
    for k in range(LAYERS):
        chosen = sel[k]
        value = feat[lax.rem(chosen, 2)]
        mine = lax.div(chosen, 2) == sec
        msk[k] = jnp.where(mine, value, jnp.zeros_like(value))
        for d in (1, 3, 2):
            xx = mod4(x + d)
            push(msk.at[k, pl.ds(m(xx * 32, 32), 32)], fx.at[k, d - 1], f1 + k * 4 + d, to_x(xx))
    target.along_z()
    target.hop()
    quarter = pl.ds(m(x * 32, 32), 32)
    other_zh = {"section": x * 2 + 1 - zh}
    for k in range(LAYERS):
        for d in (1, 3, 2):
            await_recv(fx.at[k, d - 1], f1 + k * 4 + d)
        fs[k] = msk[k, quarter] + fx[k, 0] + fx[k, 1] + fx[k, 2]
        push(fs.at[k], fz.at[k], f2 + k, other_zh)
    target.hop_z()
    for k in range(LAYERS):
        await_recv(fz.at[k], f2 + k)
        fall[y, k, quarter] = fs[k] + fz[k]
        block = fall.at[y, k, quarter]
        for d in (1, 3, 2):
            push(block, block, f3 + k * 4 + d, to_x(mod4(x + d)))
            if k:
                push(block, block, f4 + k * 4 + d, to_y(mod4(y + d)))
    for g in range(2):
        target.await_z(g)
        target.along_x(g, (1, 3))
        target.own_over(g)

    loads[2].wait()
    for k in range(LAYERS):
        for d in (1, 3, 2):
            xx = mod4(x - d)
            await_recv(fall.at[y, k, pl.ds(m(xx * 32, 32), 32)], f3 + k * 4 + d)
        if k == 0:
            for d in (1, 3, 2):
                push(fall.at[y, 0], fall.at[y, 0], f4 + d, to_y(mod4(y + d)))

        @pl.loop(0, 4)
        def _(n, k=k):
            cols = pl.ds(m(n * 256, 256), 256)
            term = nn(fall[y, k], w[k, :, cols])
            if k:
                part[n, 0] = part[n, 0] + term[:, :128]
                part[n, 1] = part[n, 1] + term[:, 128:]
            else:
                part[n, 0] = term[:, :128]
                part[n, 1] = term[:, 128:]

    r1, r2 = sems(1), sems(4)
    push(part.at[:, oc], pc, r1, sibling)
    await_recv(pc, r1)
    for d in (2, 1, 3, 0):
        v = mod4(zl + d)
        part[v, c] = part[v, c] + pc[v]
        remote = off_x if d == 0 else None
        push(part.at[v, c], pz.at[zl], r2 + d, there(zh * 4 + v), rsem=r2 + zl, when=remote)

    @pl.when(jnp.logical_not(off_x))
    def _():
        pz[zl] = part[zl, c]

    for d in range(4):
        v = mod4(zl + d)
        await_recv(pz.at[v], r2 + v, when=off_x if d == 0 else None)
    uni[...] = pz[0] + pz[1] + pz[2] + pz[3]
    h_d[group, z, :, half_c] = uni[...].astype(BF)
    draft.along_z()
    draft.hop()
    s_c, s_z, s_a, s_x = sems(1), sems(8), sems(1), sems(4)
    squares = jnp.sum(uni[...] * uni[...], axis=1, keepdims=True)
    ssc[0] = jnp.broadcast_to(squares, (128, 128)).T[0:8]
    push(ssc.at[0], ssc.at[1], s_c, sibling)
    t2 = sems(2)
    for h in range(2):
        src = uni.at[pl.ds(h * 64, 64), :]
        push(src, ur.at[:, half_c], t2 + h, turned(h), rsem=t2 + c,
             when=jnp.logical_or(off_z, c != h))

    @pl.when(jnp.logical_not(off_z))
    def _():
        ur[:, half_c] = uni[pl.ds(m(c * 64, 64), 64), :]

    await_recv(ssc.at[1], s_c)
    ssz[0] = ssc[0] + ssc[1]
    for d in range(1, 8):
        push(ssz.at[0], ssz.at[d], s_z + d, to_z(lax.rem(z + d, 8)))
    draft.hop_z()
    target.hop_over()
    for g in range(2):
        for e in (1, 3):
            target.over(g, e)
    for e in range(4):
        target.finish(e)
    loads[3].wait()
    logits_t.product((0, 1, 3, 2))
    for g in range(2):
        draft.await_z(g)
        draft.along_x(g, (1, 3))
        draft.own_over(g)
    for e in (0, 1, 3, 2):
        logits_t.send(e)
    for d in range(1, 8):
        await_recv(ssz.at[d], s_z + d)
    total = ssz[0]
    for d in range(1, 8):
        total = total + ssz[d]
    ssa[0] = total
    push(ssa.at[0], ssa.at[1], s_a, back_to(z), when=off_x)
    draft.finish(0)
    logits_d.product((0,))
    logits_d.send(0)
    for g in range(2):
        for e in (1, 3):
            draft.over(g, e)
    draft.hop_over()
    await_recv(ssa.at[1], s_a, when=off_x)
    ssx[0] = jnp.where(off_x, ssa[1], ssa[0])
    for d in range(1, 4):
        push(ssx.at[0], ssx.at[d], s_x + d, to_x(mod4(x + d)))

    def foreign(e):
        yy = mod4(y - e)
        for k in (1, 2):
            await_recv(fall.at[yy, k, quarter], f4 + k * 4 + e)
        block = fall.at[yy, pl.ds(1, 2), quarter]
        for d in (1, 3, 2):
            push(block, block, f5 + (e - 1) * 4 + d, to_x(mod4(x + d)))

    foreign(1)
    foreign(3)
    draft.finish(1)
    draft.finish(3)
    logits_d.product((1, 3))
    logits_d.send(1)
    logits_d.send(3)
    draft.finish(2)
    logits_d.product((2,))
    logits_d.send(2)
    foreign(2)
    def transpose(b):
        @pl.loop(0, LAYERS)
        def _(k):
            for i in range(4):
                ft[b, k, pl.ds(i * 256, 256)] = fall[b, k, :, pl.ds(i * 256, 256)].T

        pltpu.make_async_copy(ft.at[b], ft_h.at[b], lsem.at[4 + b]).start()

    transpose(y)
    logits_t.finish(tcol, jnp.zeros((8, 128), F32))

    @pl.loop(0, 4)
    def _(i):
        rows = pl.ds(m(i * 32, 32), 32)
        zt[rows] = logits_t.total(tcol, rows)

    for d in range(1, 4):
        await_recv(ssx.at[d], s_x + d)
    scale_rows = lax.rsqrt((ssx[0] + ssx[1] + ssx[2] + ssx[3]) / D + EPS)
    logits_d.finish(scol, scale_rows)

    @pl.loop(0, 4)
    def _(i):
        rows = pl.ds(m(i * 32, 32), 32)
        a = zt[rows]
        b = logits_d.total(scol, rows) * scol[rows, 0:1]
        zd[rows] = b
        ma = jnp.max(a, axis=1, keepdims=True)
        mb = jnp.max(b, axis=1, keepdims=True)
        ea, eb = jnp.exp(a - ma), jnp.exp(b - mb)

        def total(v):
            return jnp.sum(v, axis=1, keepdims=True)

        values = [ma, total(ea), total(ea * (a - b)), total(ea * b), mb, total(eb), total(eb * b)]
        spot = lax.broadcasted_iota(jnp.int32, (32, 128), 1)
        out = jnp.zeros((32, 128), F32)
        for j, v in enumerate(values):
            out = jnp.where(spot == j, v, out)
        stat[rows] = out

    q_c, q_f, q_e, q_y = sems(1), sems(16), sems(1), sems(4)
    stc[0] = stat[...].T[0:8]
    push(stc.at[0], stc.at[1], q_c, sibling)
    await_recv(stc.at[1], q_c)
    stz[...] = combine([stc[0], stc[1]])
    for d in range(4):
        for j in range(4):
            push(stz, stx.at[d, j], q_f + d * 4 + j, far(d, j), when=c == 1 if d + j == 0 else None)

    @pl.when(c == 0)
    def _():
        stx[0, 0] = stz[...]

    for d in range(4):
        for j in range(4):
            await_recv(stx.at[d, j], q_f + d * 4 + j, when=c == 1 if d + j == 0 else None)
    ste[0] = combine([stx[d, j] for d in range(4) for j in range(4)])
    push(ste.at[0], ste.at[1], q_e, sibling)
    await_recv(ste.at[1], q_e)
    all_stats = combine([ste[0], ste[1]])
    log_t = all_stats[0:1] + jnp.log(all_stats[1:2])
    log_d = all_stats[4:5] + jnp.log(all_stats[5:6])
    kl_o[...] = all_stats[2:3] / all_stats[1:2] - log_t + log_d
    energy = all_stats[6:7] / all_stats[5:6] - all_stats[3:4] / all_stats[1:2]
    row = lax.broadcasted_iota(jnp.int32, (8, 128), 0)
    tile = jnp.where(row == 0, log_t, jnp.where(row == 1, log_d, jnp.where(row == 2, scale_rows[0:1], energy)))
    fin[y] = tile
    fcol[...] = rows_to_cols(tile)

    @pl.loop(0, 4)
    def _(i):
        rows = pl.ds(m(i * 32, 32), 32)
        pt = jnp.exp(zt[rows] - fcol[rows, 0:1])
        pd = jnp.exp(zd[rows] - fcol[rows, 1:2])
        dall[y, rows] = (pd - pt).astype(BF)

    d1 = sems(4)
    for d in (1, 3, 2):
        push(dall.at[y], dall.at[y], d1 + d, to_y(mod4(y + d)))
    for d in range(1, 4):
        push(fin.at[y], fin.at[y], q_y + d, to_y(mod4(y + d)))

    b_c, b_x, b_z = sems(4), sems(16), sems(8)

    def product(rels):
        for rel in rels:
            if rel:
                b = mod4(y + rel)
                await_recv(dall.at[b], d1 + 4 - rel)

        @pl.loop(0, 8)
        def _(n):
            cols = pl.ds(m(n * 256, 256), 256)
            left = jnp.concatenate([dall[mod4(y + rel)] for rel in rels], axis=0)
            out = nn(left, head[:, cols]).astype(BF)
            for j, rel in enumerate(rels):
                bk[rel, :, cols] = out[j * 128:(j + 1) * 128]

        for rel in rels:
            push(bk.at[rel, pl.ds(m(oc * 64, 64), 64)], rc.at[rel], b_c + rel, sibling)

    def over_core(rel):
        await_recv(rc.at[rel], b_c + rel)
        mine = pl.ds(m(c * 64, 64), 64)
        for n in range(8):
            cols = pl.ds(n * 256, 256)
            s = bk[rel, mine, cols].astype(F32) + rc[rel, :, cols].astype(F32)
            bx[rel, n % 4, n // 4] = s.astype(BF)
        for d in (1, 3, 2):
            xx = mod4(x + d)
            push(bx.at[rel, mod4(xx - y)], rx.at[rel, d - 1], b_x + rel * 4 + d, to_x(xx))

    def over_x(rel):
        b = mod4(y + rel)
        for d in (1, 3, 2):
            await_recv(rx.at[rel, d - 1], b_x + rel * 4 + d)
        s = bx[rel, group].astype(F32)
        for d in range(3):
            s = s + rx[rel, d].astype(F32)
        bs[rel] = s.astype(BF)
        for g in range(2):
            zz = g * 4 + b
            push(bs.at[rel, g], rz.at[z], b_z + rel * 2 + g, to_z(zz), rsem=b_z + z, when=zz != z)

            @pl.when(zz == z)
            def _():
                rz[z] = bs[rel, g]

    product((0,))
    over_core(0)
    product((1, 3))
    over_core(1)
    over_core(3)
    over_x(0)
    product((2,))
    over_core(2)
    over_x(1)
    over_x(3)
    over_x(2)

    for d in range(1, 4):
        await_recv(fin.at[mod4(y - d)], q_y + d)
    gcol[...] = rows_to_cols(fin[zl])
    await_recv(ur.at[:, pl.ds(0, 128)], t2, when=jnp.logical_or(off_z, c != 0))
    await_recv(ur.at[:, pl.ds(128, 128)], t2 + 1, when=jnp.logical_or(off_z, c != 1))
    for e in (1, 3, 2):
        yy = mod4(y - e)
        await_recv(fall.at[yy, 0], f4 + e)
        for d in (1, 3, 2):
            xx = mod4(x - d)
            await_recv(fall.at[yy, pl.ds(1, 2), pl.ds(m(xx * 32, 32), 32)], f5 + (e - 1) * 4 + d)
        transpose(yy)
    for d in range(1, 8):
        zz = lax.rem(z + d, 8)
        await_recv(rz.at[zz], b_z + zz)
    total = rz[0].astype(F32)
    for j in range(1, 8):
        total = total + rz[j].astype(F32)
    bsum[...] = total.astype(BF)
    t1 = sems(1)
    push(bsum, bturn, t1, back_to(z), when=off_x)

    @pl.when(jnp.logical_not(off_x))
    def _():
        bturn[...] = bsum[...]

    await_recv(bturn, t1, when=off_x)
    bt = bturn[...].astype(F32)
    mine = pl.ds(m(c * 64, 64), 64)
    scale = gcol[mine, 2:3]
    gu[zl, c] = (scale * (bt - ur[...] * (scale * gcol[mine, 3:4] / D))).astype(BF)

    g1, g2 = sems(4), sems(4)
    for d in (0, 1, 3, 2):
        if d:
            block = gu.at[zl, c]
            push(block, block, g1 + d, {"tp": mod4(zl + d) * 2 + c})
    for d in (0, 1, 3, 2):
        v = mod4(zl - d)
        block = gu.at[v, c]
        if d:
            await_recv(block, g1 + d)
        push(block, block, g2 + d, sibling)
    for d in (0, 1, 3, 2):
        await_recv(gu.at[mod4(zl - d), oc], g2 + d)

    store = pltpu.make_async_copy(gu, gu_h, lsem.at[8])
    store.start()
    for end in ends:
        end()
    store.wait()
    for b in range(4):
        pltpu.make_async_copy(ft.at[b], ft_h.at[b], lsem.at[4 + b]).wait()


def outer(ft, gu, loss, out, loss_out):
    left = jnp.concatenate([ft[b, 0] for b in range(4)], axis=1)
    right = jnp.concatenate([gu[b, h] for b in range(4) for h in range(2)], axis=0)
    out[0] = nn(left, right).astype(BF)
    loss_out[...] = loss[...]


def per_device(features, selected, target_hidden, unite_weight, head_weight):
    def vm(shape, kind):
        return pltpu.VMEM(shape, kind)

    scratch = [
        vm((2, 128, 1024), BF), vm((128, 128), BF), vm((3, 1024, 1024), BF), vm((1024, 2048), BF),
        vm((3, 128, 1024), BF), vm((3, 3, 32, 1024), BF), vm((3, 32, 1024), BF), vm((3, 32, 1024), BF),
        vm((4, 3, 128, 1024), BF), vm((4, 3, 1024, 128), BF),
        vm((4, 2, 128, 128), F32), vm((4, 128, 128), F32), vm((4, 128, 128), F32), vm((128, 128), F32),
        vm((2, 8, 128), F32), vm((8, 8, 128), F32), vm((2, 8, 128), F32), vm((4, 8, 128), F32),
        vm((128, 128), F32), vm((128, 128), F32),
        vm((4, 8, 128, 256), BF), vm((4, 8, 128, 256), BF),
        vm((4, 128, 1024), F32), vm((4, 128, 1024), F32),
        vm((4, 128, 1024), jnp.int16), vm((4, 128, 1024), jnp.int16),
        vm((4, 128, 1024), jnp.int16), vm((4, 128, 1024), jnp.int16), vm((128, 128), F32),
        vm((4, 8, 128), F32), vm((4, 8, 128), F32), vm((4, 8, 128), F32), vm((4, 8, 128), F32),
        vm((128, 1024), F32), vm((128, 1024), F32), vm((128, 128), F32),
        vm((2, 8, 128), F32), vm((8, 128), F32), vm((4, 4, 8, 128), F32), vm((2, 8, 128), F32),
        vm((4, 8, 128), F32), vm((128, 128), F32), vm((4, 128, 1024), BF),
        vm((4, 128, 2048), BF), vm((4, 64, 2048), BF), vm((4, 4, 2, 64, 256), BF),
        vm((4, 3, 2, 64, 256), BF), vm((8, 64, 256), BF), vm((4, 2, 64, 256), BF),
        vm((64, 256), BF), vm((64, 256), BF), vm((64, 256), F32), vm((128, 128), F32),
        vm((4, 2, 64, 256), BF),
        pltpu.SemaphoreType.DMA((9,)), pltpu.SemaphoreType.DMA((NSEM,)), pltpu.SemaphoreType.DMA((NSEM,)),
    ]
    anywhere = pl.BlockSpec(memory_space=pl.ANY)
    turned, grad_united, loss = pl.pallas_call(
        kernel,
        out_shape=(
            jax.ShapeDtypeStruct((4, 3, 1024, 128), BF),
            jax.ShapeDtypeStruct((4, 2, 64, 256), BF),
            jax.ShapeDtypeStruct((1, 128), F32),
        ),
        in_specs=[pl.BlockSpec(memory_space=pltpu.SMEM)] + [anywhere] * 4,
        out_specs=(anywhere, anywhere, pl.BlockSpec(memory_space=pltpu.VMEM)),
        scratch_shapes=scratch,
        compiler_params=pltpu.CompilerParams(
            collective_id=0, has_side_effects=True, vmem_limit_bytes=58 * 1024 * 1024
        ),
    )(selected, features, target_hidden, unite_weight, head_weight)
    grad, loss = pl.pallas_call(
        outer,
        grid=(LAYERS,),
        out_shape=(
            jax.ShapeDtypeStruct((3, 1024, 256), BF),
            jax.ShapeDtypeStruct((1, 128), F32),
        ),
        in_specs=[
            pl.BlockSpec((4, 1, 1024, 128), lambda k: (0, k, 0, 0)),
            pl.BlockSpec((4, 2, 64, 256), lambda k: (0, 0, 0, 0)),
            pl.BlockSpec((1, 128), lambda k: (0, 0)),
        ],
        out_specs=(
            pl.BlockSpec((1, 1024, 256), lambda k: (k, 0, 0)),
            pl.BlockSpec((1, 128), lambda k: (0, 0)),
        ),
        compiler_params=pltpu.CompilerParams(vmem_limit_bytes=60 * 1024 * 1024),
    )(turned, grad_united, loss)
    return grad, loss.reshape(128)


def solution(mesh):
    placed = (
        P("section", "dp", "tp"),
        P(),
        P("dp", ("section", "tp")),
        P(None, "tp", "section"),
        P(("section", "tp"), "dp"),
    )
    return jax.shard_map(
        per_device,
        mesh=mesh,
        in_specs=placed,
        out_specs=(P(None, "tp", ("section", "dp")), P("dp")),
        check_vma=False,
    )
```

```python
import jax
import jax.numpy as jnp
from jax import lax
from jax.experimental import pallas as pl
from jax.experimental.pallas import tpu as pltpu
from jax.sharding import PartitionSpec as P

D = 8192
LAYERS = 3
EPS = 1e-05
BF = jnp.bfloat16
F32 = jnp.float32
NSEM = 256


def nt(a, b):
    return lax.dot_general(a, b, (((1,), (1,)), ((), ())), preferred_element_type=F32)


def nn(a, b):
    return jnp.dot(a, b, preferred_element_type=F32)


def rows_to_cols(tile):
    return jnp.concatenate([tile, jnp.zeros((120, 128), F32)], axis=0).T


def combine(parts):
    row = lax.broadcasted_iota(jnp.int32, (8, 128), 0)
    upper = row < 4

    def spread(p):
        return jnp.where(upper, p[0:1, :], p[4:5, :])

    peaks = [spread(p) for p in parts]
    peak = peaks[0]
    for other in peaks[1:]:
        peak = jnp.maximum(peak, other)
    total = jnp.zeros((8, 128), F32)
    for p, mine in zip(parts, peaks):
        total = total + p * jnp.exp(mine - peak)
    return jnp.where((row == 0) | (row == 4), peak, total)


def kernel(
    sel, feat_h, tgt_h, w_h, head_h, ft_h, gu_h, kl_o,
    feat, tgt, w, head, msk, fx, fs, fz, fall, ft,
    part, pc, pz, uni, ssc, ssz, ssa, ssx, scol, tcol,
    h_t, h_d, lp_t, lp_d, lq_t, lq_d, rq_t, rq_d, sm, sq_t, sq_d, rs_t, rs_d,
    zt, zd, stat, stc, stz, stx, ste, fin, fcol, dall,
    bk, rc, bx, rx, rz, bs, bsum, bturn, ur, gcol, gu,
    lsem, send, recv,
):
    sec = lax.axis_index("section")
    y = lax.axis_index("dp")
    tp = lax.axis_index("tp")
    x, zh = lax.div(sec, 2), lax.rem(sec, 2)
    zl, c = lax.div(tp, 2), lax.rem(tp, 2)
    z = zh * 4 + zl
    oc = 1 - c

    def mod4(v):
        return lax.rem(v + 8, 4)

    def to_x(v):
        return {"section": v * 2 + zh}

    def to_y(v):
        return {"dp": v}

    def to_z(v):
        return {"section": x * 2 + lax.div(v, 4), "tp": lax.rem(v, 4) * 2 + c}

    sibling = {"tp": zl * 2 + oc}
    group = mod4(x - y)

    def there(v):
        return {"section": mod4(x + y) * 2 + lax.div(v, 4), "dp": x, "tp": lax.rem(v, 4) * 2 + c}

    def back_to(v):
        return {"section": y * 2 + lax.div(v, 4), "dp": group, "tp": lax.rem(v, 4) * 2 + c}

    def far(d, j):
        zz = lax.rem(z + c + 2 * j, 8)
        return {"section": mod4(x + d) * 2 + lax.div(zz, 4), "tp": lax.rem(zz, 4) * 2 + c}

    def turned(h):
        return {"section": y * 2 + zh, "dp": zl, "tp": group * 2 + h}

    def turned_back(h):
        return {"section": mod4(x + zl) * 2 + zh, "dp": x, "tp": y * 2 + h}

    counter = [0]

    def sems(n):
        base = counter[0]
        counter[0] += n
        assert counter[0] <= NSEM
        return base

    ends = []

    def copy(src, dst, sem, dev, rsem=None):
        return pltpu.make_async_remote_copy(
            src_ref=src, dst_ref=dst, send_sem=send.at[sem],
            recv_sem=recv.at[sem if rsem is None else rsem],
            device_id=dev, device_id_type=pl.DeviceIdType.MESH,
        )

    def push(src, dst, sem, dev, rsem=None, when=None):
        if when is None:
            copy(src, dst, sem, dev, rsem).start()
            ends.append(lambda: copy(src, dst, sem, dev, rsem).wait_send())
        else:
            def go():
                copy(src, dst, sem, dev, rsem).start()

            def end():
                copy(src, dst, sem, dev, rsem).wait_send()

            pl.when(when)(go)
            ends.append(lambda: pl.when(when)(end))

    def await_recv(dst, sem, when=None):
        def go():
            copy(dst, dst, 0, sibling, sem).wait_recv()

        if when is None:
            go()
        else:
            pl.when(when)(go)

    def m(v, k):
        return pl.multiple_of(v, k)

    half_c = pl.ds(m(c * 128, 128), 128)
    half_o = pl.ds(m(oc * 128, 128), 128)

    loads = [
        pltpu.make_async_copy(feat_h, feat, lsem.at[0]),
        pltpu.make_async_copy(tgt_h, tgt, lsem.at[1]),
        pltpu.make_async_copy(w_h, w, lsem.at[2]),
        pltpu.make_async_copy(head_h, head, lsem.at[3]),
    ]
    for load in loads:
        load.start()

    barrier = pltpu.get_barrier_semaphore()

    def greet(dev):
        pl.semaphore_signal(barrier, inc=1, device_id=dev, device_id_type=pl.DeviceIdType.MESH)

    for d in range(1, 4):
        greet(to_x(mod4(x + d)))
        greet(to_y(mod4(y + d)))
    for d in range(1, 8):
        greet(to_z(lax.rem(z + d, 8)))
    greet(sibling)
    off_x = jnp.logical_or(x != 0, y != 0)
    off_z = jnp.logical_or(off_x, zl != 0)

    @pl.when(off_x)
    def _():
        for v in range(4):
            greet(there(zh * 4 + v))
            greet(back_to(zh * 4 + v))

    @pl.when(off_z)
    def _():
        for h in range(2):
            greet(turned(h))
            greet(turned_back(h))

    @pl.when(c == 0)
    def _():
        for d in range(1, 4):
            for j in range(1, 4):
                greet(far(d, j))

    @pl.when(c == 1)
    def _():
        for d in range(1, 4):
            for j in range(4):
                greet(far(d, j))

    pl.semaphore_wait(
        barrier, 23 + 3 * c + jnp.where(off_x, 8, 0) + jnp.where(off_z, 4, 0)
    )

    class Gather:
        def __init__(self, hid, own):
            self.hid, self.own = hid, own
            self.s1, self.sz, self.sx = sems(1), sems(8), sems(8)
            self.so, self.sf = sems(2), sems(8)
            self.s2, self.sz2 = sems(1), sems(8)

        def turn(self):
            hid, own = self.hid, self.own
            push(own, hid.at[y, z, :, half_c], self.s1, there(z), when=off_x)

            @pl.when(jnp.logical_not(off_x))
            def _():
                hid[group, z, :, half_c] = own[...]

        def along_z(self):
            mine = self.hid.at[group, z, :, half_c]
            if self.own is not None:
                await_recv(mine, self.s1, when=off_x)
            for d in range(1, 8):
                push(mine, mine, self.sz + d, to_z(lax.rem(z + d, 8)))

        def hop(self):
            piece = self.hid.at[group, z, :, half_c]
            push(piece, piece, self.s2, to_x(mod4(x + 2)))

        def hop_z(self):
            piece = self.hid.at[mod4(group + 2), z, :, half_c]
            await_recv(piece, self.s2)
            for d in range(1, 8):
                push(piece, piece, self.sz2 + d, to_z(lax.rem(z + d, 8)))

        def hop_over(self):
            for d in range(1, 8):
                await_recv(self.hid.at[mod4(group + 2), lax.rem(z + 8 - d, 8), :, half_c], self.sz2 + d)
            for g in range(2):
                block = self.block(2, g, half_c)
                push(block, block, self.sf + g * 4 + 2, sibling)

        def block(self, e, g, half):
            base = zh * 4 if g == 0 else 4 - zh * 4
            return self.hid.at[mod4(group + e), pl.ds(base, 4), :, half]

        def await_z(self, g):
            base = zh * 4 if g == 0 else 4 - zh * 4
            for j in range(1 if g == 0 else 0, 4):
                zz = base + mod4(zl + j)
                await_recv(self.hid.at[group, zz, :, half_c], self.sz + lax.rem(z - zz + 8, 8))

        def along_x(self, g, steps):
            block = self.block(0, g, half_c)
            for d in steps:
                push(block, block, self.sx + g * 4 + d, to_x(mod4(x + d)))

        def own_over(self, g):
            block = self.block(0, g, half_c)
            push(block, block, self.so + g, sibling)

        def over(self, g, e):
            block = self.block(e, g, half_c)
            await_recv(block, self.sx + g * 4 + 4 - e)
            push(block, block, self.sf + g * 4 + e, sibling)

        def finish(self, e):
            for g in range(2):
                await_recv(self.block(e, g, half_o), self.sf + g * 4 + e if e else self.so + g)

    class Logits:
        def __init__(self, hid, lp, lq, rq, sq, rs):
            self.hid, self.lp, self.lq, self.rq, self.sq, self.rs = hid, lp, lq, rq, sq, rs
            self.s, self.ss = sems(4), sems(4)

        def product(self, steps):
            hid, lp = self.hid, self.lp

            @pl.loop(0, 4)
            def _(n):
                cols = pl.ds(m(n * 256, 256), 256)
                left = jnp.concatenate(
                    [jnp.concatenate([hid[mod4(group + e), i] for i in range(8)], axis=1) for e in steps],
                    axis=0,
                )
                out = nt(left, head[cols, :])
                for j, e in enumerate(steps):
                    lp[e, :, cols] = out[j * 128:(j + 1) * 128]

        def send(self, e):
            lp, lq, sq = self.lp, self.lq, self.sq
            b = mod4(group + e)

            @pl.when(b != y)
            def _():
                @pl.loop(0, 4)
                def _(i):
                    rows = pl.ds(m(i * 32, 32), 32)
                    v = lp[e, rows]
                    peak = jnp.maximum(jnp.max(jnp.abs(v), axis=1, keepdims=True), 1e-30)
                    lq[e, rows] = jnp.round(v * (32767.0 / peak)).astype(jnp.int32).astype(jnp.int16)
                    sm[rows] = jnp.broadcast_to(peak / 32767.0, (32, 128))

                sq[e] = sm[...].T[0:8]

            push(lq.at[e], self.rq.at[y], self.s + e, to_y(b), rsem=self.s + y, when=b != y)
            push(sq.at[e], self.rs.at[y], self.ss + e, to_y(b), rsem=self.ss + y, when=b != y)

        def finish(self, col, other):
            row = lax.broadcasted_iota(jnp.int32, (8, 128), 0)
            tile = other
            for e in (1, 3, 2):
                yy = mod4(y - e)
                await_recv(self.rs.at[yy], self.ss + yy)
                tile = jnp.where(row == e, self.rs[yy], tile)
            col[...] = rows_to_cols(tile)
            for e in (1, 3, 2):
                yy = mod4(y - e)
                await_recv(self.rq.at[yy], self.s + yy)

        def total(self, col, rows):
            out = self.lp[mod4(y - group), rows]
            for e in (1, 3, 2):
                term = self.rq[mod4(y - e), rows].astype(jnp.int32).astype(F32)
                out = out + term * col[rows, e:e + 1]
            return out

    target = Gather(h_t, tgt)
    draft = Gather(h_d, None)
    logits_t = Logits(h_t, lp_t, lq_t, rq_t, sq_t, rs_t)
    logits_d = Logits(h_d, lp_d, lq_d, rq_d, sq_d, rs_d)

    loads[1].wait()
    target.turn()
    loads[0].wait()
    f1, f2, f3, f4, f5 = sems(12), sems(3), sems(12), sems(12), sems(12)
    for k in range(LAYERS):
        chosen = sel[k]
        value = feat[lax.rem(chosen, 2)]
        mine = lax.div(chosen, 2) == sec
        msk[k] = jnp.where(mine, value, jnp.zeros_like(value))
        for d in (1, 3, 2):
            xx = mod4(x + d)
            push(msk.at[k, pl.ds(m(xx * 32, 32), 32)], fx.at[k, d - 1], f1 + k * 4 + d, to_x(xx))
    quarter = pl.ds(m(x * 32, 32), 32)
    other_zh = {"section": x * 2 + 1 - zh}
    for k in range(LAYERS):
        for d in (1, 3, 2):
            await_recv(fx.at[k, d - 1], f1 + k * 4 + d)
        fs[k] = msk[k, quarter] + fx[k, 0] + fx[k, 1] + fx[k, 2]
        push(fs.at[k], fz.at[k], f2 + k, other_zh)
    target.along_z()
    target.hop()
    for k in range(LAYERS):
        await_recv(fz.at[k], f2 + k)
        fall[y, k, quarter] = fs[k] + fz[k]
        block = fall.at[y, k, quarter]
        for d in (1, 3, 2):
            push(block, block, f3 + k * 4 + d, to_x(mod4(x + d)))
            if k:
                push(block, block, f4 + k * 4 + d, to_y(mod4(y + d)))
    target.hop_z()

    loads[2].wait()
    for k in range(LAYERS):
        for d in (1, 3, 2):
            xx = mod4(x - d)
            await_recv(fall.at[y, k, pl.ds(m(xx * 32, 32), 32)], f3 + k * 4 + d)
        if k == 0:
            for d in (1, 3, 2):
                push(fall.at[y, 0], fall.at[y, 0], f4 + d, to_y(mod4(y + d)))

        def unite(n, k):
            cols = pl.ds(m(n * 256, 256), 256)
            term = nn(fall[y, k], w[k, :, cols])
            if k:
                part[n, 0] = part[n, 0] + term[:, :128]
                part[n, 1] = part[n, 1] + term[:, 128:]
            else:
                part[n, 0] = term[:, :128]
                part[n, 1] = term[:, 128:]

        if k < LAYERS - 1:
            pl.loop(0, 4)(lambda n, k=k: unite(n, k))

    r1, r2 = sems(4), sems(4)
    for d in (2, 1, 3, 0):
        v = mod4(zl + d)
        unite(v, LAYERS - 1)
        push(part.at[v, oc], pc.at[v], r1 + d, sibling)
    for d in (2, 1, 3, 0):
        v = mod4(zl + d)
        await_recv(pc.at[v], r1 + d)
        part[v, c] = part[v, c] + pc[v]
        remote = off_x if d == 0 else None
        push(part.at[v, c], pz.at[zl], r2 + d, there(zh * 4 + v), rsem=r2 + zl, when=remote)

    @pl.when(jnp.logical_not(off_x))
    def _():
        pz[zl] = part[zl, c]

    for g in range(2):
        target.await_z(g)
        target.along_x(g, (1, 3))
        target.own_over(g)
    loads[3].wait()
    target.finish(0)
    logits_t.product((0,))
    logits_t.send(0)
    for d in range(4):
        v = mod4(zl + d)
        await_recv(pz.at[v], r2 + v, when=off_x if d == 0 else None)
    uni[...] = pz[0] + pz[1] + pz[2] + pz[3]
    h_d[group, z, :, half_c] = uni[...].astype(BF)
    draft.along_z()
    draft.hop()
    s_c, s_z, s_a, s_x = sems(1), sems(8), sems(1), sems(4)
    squares = jnp.sum(uni[...] * uni[...], axis=1, keepdims=True)
    ssc[0] = jnp.broadcast_to(squares, (128, 128)).T[0:8]
    push(ssc.at[0], ssc.at[1], s_c, sibling)
    await_recv(ssc.at[1], s_c)
    ssz[0] = ssc[0] + ssc[1]
    for d in range(1, 8):
        push(ssz.at[0], ssz.at[d], s_z + d, to_z(lax.rem(z + d, 8)))
    draft.hop_z()
    target.hop_over()
    for g in range(2):
        for e in (1, 3):
            target.over(g, e)
    for e in (1, 3, 2):
        target.finish(e)
    logits_t.product((1, 3, 2))
    for g in range(2):
        draft.await_z(g)
        draft.along_x(g, (1, 3))
        draft.own_over(g)
    for e in (1, 3, 2):
        logits_t.send(e)
    for d in range(1, 8):
        await_recv(ssz.at[d], s_z + d)
    total = ssz[0]
    for d in range(1, 8):
        total = total + ssz[d]
    ssa[0] = total
    push(ssa.at[0], ssa.at[1], s_a, back_to(z), when=off_x)
    draft.finish(0)
    logits_d.product((0,))
    logits_d.send(0)
    draft.hop_over()
    draft.finish(2)
    logits_d.product((2,))
    logits_d.send(2)
    for g in range(2):
        for e in (1, 3):
            draft.over(g, e)
    await_recv(ssa.at[1], s_a, when=off_x)
    ssx[0] = jnp.where(off_x, ssa[1], ssa[0])
    for d in range(1, 4):
        push(ssx.at[0], ssx.at[d], s_x + d, to_x(mod4(x + d)))

    def foreign(e):
        yy = mod4(y - e)
        for k in (1, 2):
            await_recv(fall.at[yy, k, quarter], f4 + k * 4 + e)
        block = fall.at[yy, pl.ds(1, 2), quarter]
        for d in (1, 3, 2):
            push(block, block, f5 + (e - 1) * 4 + d, to_x(mod4(x + d)))

    foreign(1)
    foreign(3)
    draft.finish(1)
    draft.finish(3)
    logits_d.product((1, 3))
    logits_d.send(1)
    logits_d.send(3)
    foreign(2)
    t2 = sems(2)
    for h in range(2):
        src = uni.at[pl.ds(h * 64, 64), :]
        push(src, ur.at[:, half_c], t2 + h, turned(h), rsem=t2 + c,
             when=jnp.logical_or(off_z, c != h))

    @pl.when(jnp.logical_not(off_z))
    def _():
        ur[:, half_c] = uni[pl.ds(m(c * 64, 64), 64), :]

    def transpose(b):
        @pl.loop(0, LAYERS)
        def _(k):
            for i in range(4):
                ft[b, k, pl.ds(i * 256, 256)] = fall[b, k, :, pl.ds(i * 256, 256)].T

        pltpu.make_async_copy(ft.at[b], ft_h.at[b], lsem.at[4 + b]).start()

    transpose(y)
    logits_t.finish(tcol, jnp.zeros((8, 128), F32))

    @pl.loop(0, 4)
    def _(i):
        rows = pl.ds(m(i * 32, 32), 32)
        zt[rows] = logits_t.total(tcol, rows)

    for d in range(1, 4):
        await_recv(ssx.at[d], s_x + d)
    scale_rows = lax.rsqrt((ssx[0] + ssx[1] + ssx[2] + ssx[3]) / D + EPS)
    logits_d.finish(scol, scale_rows)

    @pl.loop(0, 4)
    def _(i):
        rows = pl.ds(m(i * 32, 32), 32)
        a = zt[rows]
        b = logits_d.total(scol, rows) * scol[rows, 0:1]
        zd[rows] = b
        ma = jnp.max(a, axis=1, keepdims=True)
        mb = jnp.max(b, axis=1, keepdims=True)
        ea, eb = jnp.exp(a - ma), jnp.exp(b - mb)

        def total(v):
            return jnp.sum(v, axis=1, keepdims=True)

        values = [ma, total(ea), total(ea * (a - b)), total(ea * b), mb, total(eb), total(eb * b)]
        spot = lax.broadcasted_iota(jnp.int32, (32, 128), 1)
        out = jnp.zeros((32, 128), F32)
        for j, v in enumerate(values):
            out = jnp.where(spot == j, v, out)
        stat[rows] = out

    q_c, q_f, q_e, q_y = sems(1), sems(16), sems(1), sems(4)
    stc[0] = stat[...].T[0:8]
    push(stc.at[0], stc.at[1], q_c, sibling)
    await_recv(stc.at[1], q_c)
    stz[...] = combine([stc[0], stc[1]])
    for d in range(4):
        for j in range(4):
            push(stz, stx.at[d, j], q_f + d * 4 + j, far(d, j), when=c == 1 if d + j == 0 else None)

    @pl.when(c == 0)
    def _():
        stx[0, 0] = stz[...]

    for d in range(4):
        for j in range(4):
            await_recv(stx.at[d, j], q_f + d * 4 + j, when=c == 1 if d + j == 0 else None)
    ste[0] = combine([stx[d, j] for d in range(4) for j in range(4)])
    push(ste.at[0], ste.at[1], q_e, sibling)
    await_recv(ste.at[1], q_e)
    all_stats = combine([ste[0], ste[1]])
    log_t = all_stats[0:1] + jnp.log(all_stats[1:2])
    log_d = all_stats[4:5] + jnp.log(all_stats[5:6])
    kl_o[...] = all_stats[2:3] / all_stats[1:2] - log_t + log_d
    energy = all_stats[6:7] / all_stats[5:6] - all_stats[3:4] / all_stats[1:2]
    row = lax.broadcasted_iota(jnp.int32, (8, 128), 0)
    tile = jnp.where(row == 0, log_t, jnp.where(row == 1, log_d, jnp.where(row == 2, scale_rows[0:1], energy)))
    fin[y] = tile
    fcol[...] = rows_to_cols(tile)

    @pl.loop(0, 4)
    def _(i):
        rows = pl.ds(m(i * 32, 32), 32)
        pt = jnp.exp(zt[rows] - fcol[rows, 0:1])
        pd = jnp.exp(zd[rows] - fcol[rows, 1:2])
        dall[y, rows] = (pd - pt).astype(BF)

    d1 = sems(4)
    near = [copy(dall.at[y], dall.at[y], d1 + d, to_y(mod4(y + d))) for d in (1, 3)]
    for sent in near:
        sent.start()
    for d in range(1, 4):
        push(fin.at[y], fin.at[y], q_y + d, to_y(mod4(y + d)))

    b_c, b_x, b_z = sems(4), sems(16), sems(8)

    def product(rels):
        for rel in rels:
            if rel:
                b = mod4(y + rel)
                await_recv(dall.at[b], d1 + 4 - rel)

        @pl.loop(0, 8)
        def _(n):
            cols = pl.ds(m(n * 256, 256), 256)
            left = jnp.concatenate([dall[mod4(y + rel)] for rel in rels], axis=0)
            out = nn(left, head[:, cols]).astype(BF)
            for j, rel in enumerate(rels):
                bk[rel, :, cols] = out[j * 128:(j + 1) * 128]

        for rel in rels:
            push(bk.at[rel, pl.ds(m(oc * 64, 64), 64)], rc.at[rel], b_c + rel, sibling)

    def over_core(rel):
        await_recv(rc.at[rel], b_c + rel)
        mine = pl.ds(m(c * 64, 64), 64)
        for n in range(8):
            cols = pl.ds(n * 256, 256)
            s = bk[rel, mine, cols].astype(F32) + rc[rel, :, cols].astype(F32)
            bx[rel, n % 4, n // 4] = s.astype(BF)
        for d in (1, 3, 2):
            xx = mod4(x + d)
            push(bx.at[rel, mod4(xx - y)], rx.at[rel, d - 1], b_x + rel * 4 + d, to_x(xx))

    def over_x(rel):
        b = mod4(y + rel)
        for d in (1, 3, 2):
            await_recv(rx.at[rel, d - 1], b_x + rel * 4 + d)
        s = bx[rel, group].astype(F32)
        for d in range(3):
            s = s + rx[rel, d].astype(F32)
        bs[rel] = s.astype(BF)
        for g in range(2):
            zz = g * 4 + b
            push(bs.at[rel, g], rz.at[z], b_z + rel * 2 + g, to_z(zz), rsem=b_z + z, when=zz != z)

            @pl.when(zz == z)
            def _():
                rz[z] = bs[rel, g]

    product((0,))
    over_core(0)
    for sent in near:
        sent.wait_send()
    push(dall.at[y], dall.at[y], d1 + 2, to_y(mod4(y + 2)))
    product((1, 3))
    over_core(1)
    over_core(3)
    over_x(0)
    product((2,))
    over_core(2)
    over_x(1)
    over_x(3)
    over_x(2)

    for d in range(1, 4):
        await_recv(fin.at[mod4(y - d)], q_y + d)
    gcol[...] = rows_to_cols(fin[zl])
    await_recv(ur.at[:, pl.ds(0, 128)], t2, when=jnp.logical_or(off_z, c != 0))
    await_recv(ur.at[:, pl.ds(128, 128)], t2 + 1, when=jnp.logical_or(off_z, c != 1))
    for e in (1, 3, 2):
        yy = mod4(y - e)
        await_recv(fall.at[yy, 0], f4 + e)
        for d in (1, 3, 2):
            xx = mod4(x - d)
            await_recv(fall.at[yy, pl.ds(1, 2), pl.ds(m(xx * 32, 32), 32)], f5 + (e - 1) * 4 + d)
        transpose(yy)
    for d in range(1, 8):
        zz = lax.rem(z + d, 8)
        await_recv(rz.at[zz], b_z + zz)
    total = rz[0].astype(F32)
    for j in range(1, 8):
        total = total + rz[j].astype(F32)
    bsum[...] = total.astype(BF)
    t1 = sems(1)
    push(bsum, bturn, t1, back_to(z), when=off_x)

    @pl.when(jnp.logical_not(off_x))
    def _():
        bturn[...] = bsum[...]

    await_recv(bturn, t1, when=off_x)
    bt = bturn[...].astype(F32)
    mine = pl.ds(m(c * 64, 64), 64)
    scale = gcol[mine, 2:3]
    gu[zl, c] = (scale * (bt - ur[...] * (scale * gcol[mine, 3:4] / D))).astype(BF)

    g1, g2 = sems(4), sems(4)
    for d in (0, 1, 3, 2):
        if d:
            block = gu.at[zl, c]
            push(block, block, g1 + d, {"tp": mod4(zl + d) * 2 + c})
    for d in (0, 1, 3, 2):
        v = mod4(zl - d)
        block = gu.at[v, c]
        if d:
            await_recv(block, g1 + d)
        push(block, block, g2 + d, sibling)
    for d in (0, 1, 3, 2):
        await_recv(gu.at[mod4(zl - d), oc], g2 + d)

    store = pltpu.make_async_copy(gu, gu_h, lsem.at[8])
    store.start()
    for end in ends:
        end()
    store.wait()
    for b in range(4):
        pltpu.make_async_copy(ft.at[b], ft_h.at[b], lsem.at[4 + b]).wait()


def outer(ft, gu, loss, out, loss_out):
    left = jnp.concatenate([ft[b, 0] for b in range(4)], axis=1)
    right = jnp.concatenate([gu[b, h] for b in range(4) for h in range(2)], axis=0)
    out[0] = nn(left, right).astype(BF)
    loss_out[...] = loss[...]


def per_device(features, selected, target_hidden, unite_weight, head_weight):
    def vm(shape, kind):
        return pltpu.VMEM(shape, kind)

    scratch = [
        vm((2, 128, 1024), BF), vm((128, 128), BF), vm((3, 1024, 1024), BF), vm((1024, 2048), BF),
        vm((3, 128, 1024), BF), vm((3, 3, 32, 1024), BF), vm((3, 32, 1024), BF), vm((3, 32, 1024), BF),
        vm((4, 3, 128, 1024), BF), vm((4, 3, 1024, 128), BF),
        vm((4, 2, 128, 128), F32), vm((4, 128, 128), F32), vm((4, 128, 128), F32), vm((128, 128), F32),
        vm((2, 8, 128), F32), vm((8, 8, 128), F32), vm((2, 8, 128), F32), vm((4, 8, 128), F32),
        vm((128, 128), F32), vm((128, 128), F32),
        vm((4, 8, 128, 256), BF), vm((4, 8, 128, 256), BF),
        vm((4, 128, 1024), F32), vm((4, 128, 1024), F32),
        vm((4, 128, 1024), jnp.int16), vm((4, 128, 1024), jnp.int16),
        vm((4, 128, 1024), jnp.int16), vm((4, 128, 1024), jnp.int16), vm((128, 128), F32),
        vm((4, 8, 128), F32), vm((4, 8, 128), F32), vm((4, 8, 128), F32), vm((4, 8, 128), F32),
        vm((128, 1024), F32), vm((128, 1024), F32), vm((128, 128), F32),
        vm((2, 8, 128), F32), vm((8, 128), F32), vm((4, 4, 8, 128), F32), vm((2, 8, 128), F32),
        vm((4, 8, 128), F32), vm((128, 128), F32), vm((4, 128, 1024), BF),
        vm((4, 128, 2048), BF), vm((4, 64, 2048), BF), vm((4, 4, 2, 64, 256), BF),
        vm((4, 3, 2, 64, 256), BF), vm((8, 64, 256), BF), vm((4, 2, 64, 256), BF),
        vm((64, 256), BF), vm((64, 256), BF), vm((64, 256), F32), vm((128, 128), F32),
        vm((4, 2, 64, 256), BF),
        pltpu.SemaphoreType.DMA((9,)), pltpu.SemaphoreType.DMA((NSEM,)), pltpu.SemaphoreType.DMA((NSEM,)),
    ]
    anywhere = pl.BlockSpec(memory_space=pl.ANY)
    turned, grad_united, loss = pl.pallas_call(
        kernel,
        out_shape=(
            jax.ShapeDtypeStruct((4, 3, 1024, 128), BF),
            jax.ShapeDtypeStruct((4, 2, 64, 256), BF),
            jax.ShapeDtypeStruct((1, 128), F32),
        ),
        in_specs=[pl.BlockSpec(memory_space=pltpu.SMEM)] + [anywhere] * 4,
        out_specs=(anywhere, anywhere, pl.BlockSpec(memory_space=pltpu.VMEM)),
        scratch_shapes=scratch,
        compiler_params=pltpu.CompilerParams(
            collective_id=0, has_side_effects=True, vmem_limit_bytes=58 * 1024 * 1024
        ),
    )(selected, features, target_hidden, unite_weight, head_weight)
    grad, loss = pl.pallas_call(
        outer,
        grid=(LAYERS,),
        out_shape=(
            jax.ShapeDtypeStruct((3, 1024, 256), BF),
            jax.ShapeDtypeStruct((1, 128), F32),
        ),
        in_specs=[
            pl.BlockSpec((4, 1, 1024, 128), lambda k: (0, k, 0, 0)),
            pl.BlockSpec((4, 2, 64, 256), lambda k: (0, 0, 0, 0)),
            pl.BlockSpec((1, 128), lambda k: (0, 0)),
        ],
        out_specs=(
            pl.BlockSpec((1, 1024, 256), lambda k: (k, 0, 0)),
            pl.BlockSpec((1, 128), lambda k: (0, 0)),
        ),
        compiler_params=pltpu.CompilerParams(vmem_limit_bytes=60 * 1024 * 1024),
    )(turned, grad_united, loss)
    return grad, loss.reshape(128)


def solution(mesh):
    placed = (
        P("section", "dp", "tp"),
        P(),
        P("dp", ("section", "tp")),
        P(None, "tp", "section"),
        P(("section", "tp"), "dp"),
    )
    return jax.shard_map(
        per_device,
        mesh=mesh,
        in_specs=placed,
        out_specs=(P(None, "tp", ("section", "dp")), P("dp")),
        check_vma=False,
    )
```
